32 devices in a mesh: dp: 8 (over z, x), pipe: 2 (over y), tensor: 2 (over core).
Axes of the slice: x: 2, y: 2, z: 4, core: 2. Of those that a mesh axis runs over, the one named last changes fastest.
Arguments:
- ends: bfloat16 [2, 196, 128, 512], P('pipe', 'tensor', 'dp'), may hold values from -6 to 6
- image_counts: int32 [8], P('dp'), may hold values from 8 to 16, as said below
- norm_gains: float32 [2, 2, 512], P('pipe'), may hold values from 0.5 to 1.5
- norm_shifts: float32 [2, 2, 512], P('pipe'), may hold values from -1.5 to 1.5
- w_qkv: bfloat16 [2, 3, 512, 512], P('pipe', None, 'dp', 'tensor'), may hold values from -0.25 to 0.25
- qv_bias: float32 [2, 2, 512], P('pipe', None, 'tensor'), may hold values from -1.5 to 1.5
- rel_table: float32 [2, 16, 169], P('pipe', 'tensor'), may hold values from -4 to 4
- w_proj: bfloat16 [2, 512, 512], P('pipe', 'dp', 'tensor'), may hold values from -0.75 to 0.75
- out_biases: float32 [2, 2, 512], P('pipe'), may hold values from -1.5 to 1.5
- w_fc1: bfloat16 [2, 512, 2048], P('pipe', 'dp', 'tensor'), may hold values from -0.25 to 0.25
- fc1_bias: float32 [2, 2048], P('pipe', 'tensor'), may hold values from -1.5 to 1.5
- w_fc2: bfloat16 [2, 512, 2048], P('pipe', 'dp', 'tensor'), may hold values from -0.125 to 0.125
Outputs:
- section_input_grads: bfloat16 [2, 196, 128, 512], P('pipe', 'tensor', 'dp')
- norm_gains_grad: float32 [2, 2, 512], P('pipe')
- norm_shifts_grad: float32 [2, 2, 512], P('pipe')
- w_qkv_grad: float32 [2, 3, 512, 512], P('pipe', None, 'dp', 'tensor')
- qv_bias_grad: float32 [2, 2, 512], P('pipe', None, 'tensor')
- rel_table_grad: float32 [2, 16, 169], P('pipe', 'tensor')
- w_proj_grad: float32 [2, 512, 512], P('pipe', 'dp', 'tensor')
- out_biases_grad: float32 [2, 2, 512], P('pipe')
- w_fc1_grad: float32 [2, 512, 2048], P('pipe', 'dp', 'tensor')
- fc1_bias_grad: float32 [2, 2048], P('pipe', 'tensor')
- w_fc2_grad: float32 [2, 512, 2048], P('pipe', 'dp', 'tensor')
The draws below stay inside these ranges and needn't reach their ends.
Inputs may be any that keep to these rules, and one draw needn't show every extreme that they name: Data shard d holds 16 image slots, of which the first image_counts[d] are real; some shard is full.
All inputs are finite; a program needn't handle non-finite values.
Results may differ from the reference program's by a relative error of at most 0.029.
Values may be sent and summed in bfloat16 or wider, within the bound.
A program may use at most 256 MiB of HBM per device.

```python
import math
import jax
import jax.numpy as jnp
from jax import lax

D = 512
HEADS = 16
HD = 32
FF = 2048
SIDE = 14
WIN = 7
SHIFT = 3
IMG_DEV = 16
IMAGES = 128
N_DP = 8


def draw_image_counts(key, part):
    low_count = (IMG_DEV + 1) // 2
    counts = jax.random.randint(jax.random.fold_in(key, 1), (N_DP,), low_count, IMG_DEV + 1)
    shuffled = jax.random.permutation(jax.random.fold_in(key, 2), N_DP)
    counts = counts.at[shuffled[0]].set(IMG_DEV)
    counts = counts.at[shuffled[1]].set(low_count)
    return counts.astype(jnp.int32)


def shard_levels(stream_key, extent, split, low, high):
    def one(dim, blocks):
        draws = jax.random.uniform(jax.random.fold_in(jax.random.fold_in(stream_key, 6), dim), (blocks,), jnp.float32, low / len(split), high / len(split))
        return jnp.repeat(jnp.exp(draws), extent[dim] // blocks).reshape((-1,) + (1,) * (len(extent) - dim - 1))

    gain = one(*split[0])
    for cut in split[1:]:
        gain = gain * one(*cut)
    return gain


def normal_values(rng, extent, scale, bound, shards=(), kind=jnp.bfloat16):
    array = jax.random.normal(rng, extent, jnp.float32) * scale
    if len(shards) > 0:
        array = shard_levels(rng, extent, shards, -0.22, 0.18) * array
    return jnp.clip(array, min=-bound, max=bound).astype(kind)


def setup_inputs(seed: int = 0) -> dict:
    keys = jax.random.split(jax.random.key(seed), 13)
    ends = normal_values(keys[0], (2, SIDE * SIDE, IMAGES, D), 1.0, 6.0, ((0, 2), (1, 2), (2, 8)))
    image_counts = draw_image_counts(jax.random.fold_in(keys[12], 71), 0)
    norm_gains = jnp.clip(1.0 + 0.1 * jax.random.normal(keys[2], (2, 2, D), jnp.float32), 0.5, 1.5)
    norm_shifts = normal_values(keys[3], (2, 2, D), 0.3, 1.5, ((0, 2),), jnp.float32)
    w_qkv = normal_values(keys[4], (2, 3, D, D), D ** -0.5, 0.25, ((0, 2), (2, 8), (3, 2)))
    qv_bias = normal_values(keys[5], (2, 2, D), 0.3, 1.5, ((0, 2), (2, 2)), jnp.float32)
    rel_table = normal_values(keys[6], (2, HEADS, (2 * WIN - 1) * (2 * WIN - 1)), 1.0, 4.0, ((0, 2), (1, 2)), jnp.float32)
    w_proj = normal_values(keys[7], (2, D, D), (D // 8) ** -0.5, 0.75, ((0, 2), (1, 8), (2, 2)))
    out_biases = normal_values(keys[8], (2, 2, D), 0.3, 1.5, ((0, 2),), jnp.float32)
    w_fc1 = normal_values(keys[9], (2, D, FF), D ** -0.5, 0.25, ((0, 2), (1, 8), (2, 2)))
    fc1_bias = normal_values(keys[10], (2, FF), 0.3, 1.5, ((0, 2), (1, 2)), jnp.float32)
    w_fc2 = normal_values(keys[11], (2, D, FF), FF ** -0.5, 0.125, ((0, 2), (1, 8), (2, 2)))
    return dict(ends=ends, image_counts=image_counts, norm_gains=norm_gains, norm_shifts=norm_shifts, w_qkv=w_qkv, qv_bias=qv_bias, rel_table=rel_table, w_proj=w_proj, out_biases=out_biases, w_fc1=w_fc1, fc1_bias=fc1_bias, w_fc2=w_fc2)


HIGHEST = lax.Precision.HIGHEST

@jax.custom_vjp
def low(v):
    return lax.optimization_barrier(v.astype(jnp.bfloat16)).astype(jnp.float32)

@jax.custom_vjp
def low_back(v):
    return v

def low_keep(v):
    return (low(v), None)

def low_pass(kept, grad):
    return (grad,)

def back_keep(v):
    return (v, None)

def back_low(kept, grad):
    return (low(grad),)
low.defvjp(low_keep, low_pass)
low_back.defvjp(back_keep, back_low)

def window_tables():
    places = jnp.arange(WIN * WIN, dtype=jnp.int32)
    rows_in = places // WIN
    cols_in = places % WIN
    rel_index = (rows_in[:, None] - rows_in[None, :] + WIN - 1) * (2 * WIN - 1) + (cols_in[:, None] - cols_in[None, :] + WIN - 1)
    per_side = SIDE // WIN
    windows = jnp.arange(per_side * per_side, dtype=jnp.int32)
    grid_row = (windows // per_side)[:, None] * WIN + rows_in[None, :]
    grid_col = (windows % per_side)[:, None] * WIN + cols_in[None, :]

    def region(position):
        return (position >= SIDE - WIN).astype(jnp.int32) + (position >= SIDE - SHIFT).astype(jnp.int32)
    labels = 3 * region(grid_row) + region(grid_col)
    region_mask = jnp.where(labels[:, :, None] != labels[:, None, :], -100.0, 0.0).astype(jnp.float32)
    return (rel_index.astype(jnp.int32), region_mask)

def layer_norm(values, gain_row, shift_row):
    center = values - lax.optimization_barrier(jnp.mean(values, axis=-1, keepdims=True))
    spread = lax.optimization_barrier(jnp.mean(center * center, axis=-1, keepdims=True))
    return center * lax.rsqrt(spread + 1e-05) * gain_row + shift_row

def block(values, weights, layer_no, offset, mask_scale, rel_index, region_mask):
    image_total = values.shape[0]
    per_side = SIDE // WIN
    normed = low(layer_norm(values, weights[0][layer_no, 0], weights[1][layer_no, 0]))
    grid_view = jnp.roll(normed.reshape(image_total, SIDE, SIDE, D), (-offset, -offset), axis=(1, 2))
    blocks = grid_view.reshape(image_total, per_side, WIN, per_side, WIN, D).transpose(0, 1, 3, 2, 4, 5)
    blocks = blocks.reshape(image_total * per_side * per_side, WIN * WIN, D)
    qkv_weight = weights[2][layer_no]
    queries = low_back(jnp.einsum('wtd,de->wte', blocks, qkv_weight[0], precision=HIGHEST) + weights[3][layer_no, 0])
    queries = low(queries * HD ** (-0.5))
    keys_in = low_back(low(jnp.einsum('wtd,de->wte', blocks, qkv_weight[1], precision=HIGHEST)))
    values_in = low_back(low(jnp.einsum('wtd,de->wte', blocks, qkv_weight[2], precision=HIGHEST) + weights[3][layer_no, 1]))
    windows_n = blocks.shape[0]
    queries = queries.reshape(windows_n, WIN * WIN, HEADS, HD)
    keys_in = keys_in.reshape(windows_n, WIN * WIN, HEADS, HD)
    values_in = values_in.reshape(windows_n, WIN * WIN, HEADS, HD)
    rel_bias = weights[4][layer_no][:, rel_index]
    tiled_mask = jnp.tile(region_mask, (image_total, 1, 1))[:, None] * mask_scale
    scores = jnp.einsum('wqhe,wkhe->whqk', queries, keys_in, precision=HIGHEST) + rel_bias[None] + tiled_mask
    scores = low_back(scores)
    attn_probs = low(jax.nn.softmax(scores, axis=-1))
    attended = jnp.einsum('whqk,wkhe->wqhe', attn_probs, values_in, precision=HIGHEST).reshape(windows_n, WIN * WIN, D)
    attended = low_back(low(attended))
    grid_view = attended.reshape(image_total, per_side, per_side, WIN, WIN, D).transpose(0, 1, 3, 2, 4, 5)
    grid_view = grid_view.reshape(image_total, SIDE, SIDE, D)
    merged = jnp.roll(grid_view, (offset, offset), axis=(1, 2)).reshape(image_total, SIDE * SIDE, D)
    branch = low_back(jnp.einsum('ntd,ed->nte', merged, weights[5][layer_no], precision=HIGHEST) + weights[6][layer_no, 0])
    middle = values + branch
    normed_two = low(layer_norm(middle, weights[0][layer_no, 1], weights[1][layer_no, 1]))
    hidden_pre = low_back(jnp.einsum('ntd,df->ntf', normed_two, weights[7][layer_no], precision=HIGHEST) + weights[8][layer_no])
    hidden = low(jax.nn.gelu(hidden_pre, approximate=False))
    branch_two = low_back(jnp.einsum('ntf,df->ntd', hidden, weights[9][layer_no], precision=HIGHEST) + weights[6][layer_no, 1])
    return middle + branch_two

def reference(ends, image_counts, norm_gains, norm_shifts, w_qkv, qv_bias, rel_table, w_proj, out_biases, w_fc1, fc1_bias, w_fc2):
    params = tuple((array_in.astype(jnp.float32) for array_in in (norm_gains, norm_shifts, w_qkv, qv_bias, rel_table, w_proj, out_biases, w_fc1, fc1_bias, w_fc2)))
    rel_index, region_mask = window_tables()
    image_ids = jnp.arange(IMAGES, dtype=jnp.int32)
    real_mask = (image_ids % IMG_DEV < image_counts[image_ids // IMG_DEV]).astype(jnp.float32)
    inputs_f = jnp.transpose(ends[0].astype(jnp.float32), (1, 0, 2))
    cotangent = jnp.transpose(ends[1].astype(jnp.float32), (1, 0, 2)) * real_mask[:, None, None]
    group_size = math.gcd(IMAGES, 16)
    steps_n = IMAGES // group_size
    grouped_in = inputs_f.reshape(steps_n, group_size, SIDE * SIDE, D)
    grouped_cot = cotangent.reshape(steps_n, group_size, SIDE * SIDE, D)

    def first_layer(values, *weights):
        return low_back(low(block(values, weights, 0, 0, 0.0, rel_index, region_mask)))

    def second_layer(values, *weights):
        return block(values, weights, 1, SHIFT, 1.0, rel_index, region_mask)

    def one_group(totals, group_pair):
        batch_in, batch_cot = group_pair
        middle, first_vjp = jax.vjp(first_layer, batch_in, *params)
        final_out, second_vjp = jax.vjp(second_layer, middle, *params)
        second_grads = second_vjp(batch_cot)
        first_grads = first_vjp(second_grads[0])
        totals = tuple((running + from_first + from_second for running, from_first, from_second in zip(totals, first_grads[1:], second_grads[1:])))
        return (totals, (first_grads[0], second_grads[0]))
    zero_grads = tuple((jnp.zeros_like(array_in) for array_in in params))
    totals, (input_grads, middle_grads) = lax.scan(one_group, zero_grads, (grouped_in, grouped_cot))
    section_grads = jnp.stack([input_grads.reshape(IMAGES, SIDE * SIDE, D), middle_grads.reshape(IMAGES, SIDE * SIDE, D)])
    section_grads = jnp.transpose(section_grads, (0, 2, 1, 3)).astype(jnp.bfloat16)
    return (section_grads, totals[0], totals[1], totals[2], totals[3], totals[4], totals[5], totals[6], totals[7], totals[8], totals[9])
```

```python
from functools import partial

import jax
import jax.numpy as jnp
import numpy as np
from jax import lax
from jax.experimental import pallas as pl
from jax.experimental.pallas import tpu as pltpu
from jax.sharding import PartitionSpec as P

D = 512
HEADS = 16
HD = 32
FF = 2048
SIDE = 14
WIN = 7
SHIFT = 3
NW = 4
WP = 64
IMG_ROWS = NW * WP
GH = 4
NG = HEADS // GH
Q_SCALE = HD ** (-0.5)
TABLE = (2 * WIN - 1) ** 2
F32 = jnp.float32
BF16 = jnp.bfloat16
HIGHEST = lax.Precision.HIGHEST
ALL_AXES = ("dp", "tensor", "pipe")


def token_order(offset):
    order = np.full((IMG_ROWS,), -1, np.int64)
    per_side = SIDE // WIN
    for win in range(NW):
        for place in range(WIN * WIN):
            row = (win // per_side) * WIN + place // WIN
            col = (win % per_side) * WIN + place % WIN
            order[win * WP + place] = ((row + offset) % SIDE) * SIDE + (col + offset) % SIDE
    return order


def one_hot_order(offset):
    order = token_order(offset)
    return (order[:, None] == np.arange(SIDE * SIDE)[None, :]).astype(np.float32)


def rel_one_hot():
    places = np.arange(WP)
    rows_in, cols_in = places // WIN, places % WIN
    index = (rows_in[None, :] - rows_in[:, None] + WIN - 1) * (2 * WIN - 1) + (
        cols_in[None, :] - cols_in[:, None] + WIN - 1
    )
    real = places < WIN * WIN
    index = np.where(real[:, None] & real[None, :], index, -1).astype(np.int32)
    return (jnp.asarray(index)[None] == jnp.arange(TABLE, dtype=jnp.int32)[:, None, None]).astype(F32)


def region_masks():
    def region(pos):
        return (pos >= SIDE - WIN).astype(np.int64) + (pos >= SIDE - SHIFT).astype(np.int64)

    per_side = SIDE // WIN
    out = np.zeros((NW, WP, WP), np.float32)
    places = np.arange(WIN * WIN)
    for win in range(NW):
        row = (win // per_side) * WIN + places // WIN
        col = (win % per_side) * WIN + places % WIN
        label = 3 * region(row) + region(col)
        out[win, : WIN * WIN, : WIN * WIN] = np.where(label[:, None] != label[None, :], -100.0, 0.0)
    return out


def score_bias(table, mask):
    hot = rel_one_hot().reshape(TABLE, WP * WP)
    bias = jnp.dot(table, hot, precision=HIGHEST).reshape(NG, GH, WP, WP)
    pad = jnp.where(jnp.arange(WP) >= WIN * WIN, -1e30, 0.0).astype(F32)
    bias = bias.transpose(0, 2, 1, 3)[None] + pad[None, None, :, None, None]
    bias = bias + jnp.asarray(mask)[:, None, :, None, :]
    return bias.reshape(mask.shape[0], NG, WP, GH * WP)


def dot(a, b, a_dim, b_dim):
    return lax.dot_general(a, b, (((a_dim,), (b_dim,)), ((), ())), preferred_element_type=F32)


def normalize(values):
    center = values - jnp.mean(values, axis=-1, keepdims=True)
    spread = jnp.mean(center * center, axis=-1, keepdims=True)
    rstd = lax.rsqrt(spread + 1e-05)
    return center * rstd, rstd


def norm_back(grad, n, rstd, gain):
    e = grad * gain
    return rstd * (
        e - jnp.mean(e, axis=-1, keepdims=True) - n * jnp.mean(e * n, axis=-1, keepdims=True)
    )


def spread_heads(block):
    lane_head = lax.broadcasted_iota(jnp.int32, block.shape, 1) // HD
    wide = block.astype(F32)
    return jnp.concatenate(
        [jnp.where(lane_head == h, wide, 0.0).astype(BF16) for h in range(GH)], axis=0
    )


def fold_heads(block):
    lane_head = lax.broadcasted_iota(jnp.int32, (WP, GH * HD), 1) // HD
    out = jnp.zeros((WP, GH * HD), F32)
    for h in range(GH):
        out = jnp.where(lane_head == h, block[h * WP : (h + 1) * WP], out)
    return out


def softmax_rows(scores):
    top = jnp.max(scores, axis=0, keepdims=True)
    part = jnp.exp(scores - top)
    return part / jnp.sum(part, axis=0, keepdims=True)


def attend(bias_ref, qkv_s, o_s, p_s):
    wins = bias_ref.shape[0]

    def one_window(win, carry):
        rows = pl.ds(pl.multiple_of(win * WP, WP), WP)
        for g in range(NG):
            lanes = slice(g * 128, (g + 1) * 128)
            q = qkv_s[rows, lanes]
            k = qkv_s[rows, D + g * 128 : D + (g + 1) * 128]
            v = qkv_s[rows, 2 * D + g * 128 : 2 * D + (g + 1) * 128]
            bias = bias_ref[win, g] if wins > 1 else bias_ref[0, g]
            p = softmax_rows(dot(k, spread_heads(q), 1, 1) + bias)
            if p_s is not None:
                p_s[win, g] = p
            o_s[rows, lanes] = fold_heads(dot(p.astype(BF16), v, 0, 0)).astype(BF16)
        return carry

    lax.fori_loop(0, NW, one_window, 0)


def attend_back(qkv_s, do_s, p_s, dqkv_ref, base, table_ref):
    def one_window(win, carry):
        rows = pl.ds(pl.multiple_of(win * WP, WP), WP)
        out_rows = pl.ds(pl.multiple_of(base + win * WP, WP), WP)
        for g in range(NG):
            lanes = slice(g * 128, (g + 1) * 128)
            k_lanes = slice(D + g * 128, D + (g + 1) * 128)
            v_lanes = slice(2 * D + g * 128, 2 * D + (g + 1) * 128)
            q_wide = spread_heads(qkv_s[rows, lanes])
            do_wide = spread_heads(do_s[rows, lanes])
            k = qkv_s[rows, k_lanes]
            v = qkv_s[rows, v_lanes]
            p = p_s[win, g]
            dp = dot(v, do_wide, 1, 1)
            ds = (p * (dp - jnp.sum(p * dp, axis=0, keepdims=True))).astype(BF16)
            table_ref[g] += ds.astype(F32)
            dqkv_ref[out_rows, lanes] = (fold_heads(dot(ds, k, 0, 0)) * Q_SCALE).astype(BF16)
            dqkv_ref[out_rows, k_lanes] = dot(ds, q_wide, 1, 0).astype(BF16)
            dqkv_ref[out_rows, v_lanes] = dot(p.astype(BF16), do_wide, 1, 0).astype(BF16)
        return carry

    lax.fori_loop(0, NW, one_window, 0)


def forward_half(x, small_ref, wqkv_ref, wproj_ref, bias_ref, qkv_s, o_s, p_s):
    n1, r1 = normalize(x)
    h = (n1 * small_ref[0:1] + small_ref[1:2]).astype(BF16)
    qkv_s[:, 0:D] = ((dot(h, wqkv_ref[0], 1, 0) + small_ref[4:5]) * Q_SCALE).astype(BF16)
    qkv_s[:, D : 2 * D] = dot(h, wqkv_ref[1], 1, 0).astype(BF16)
    qkv_s[:, 2 * D : 3 * D] = (dot(h, wqkv_ref[2], 1, 0) + small_ref[5:6]).astype(BF16)
    attend(bias_ref, qkv_s, o_s, p_s)
    o = o_s[...]
    x1 = x + (dot(o, wproj_ref[...], 1, 1) + small_ref[6:7])
    n2, r2 = normalize(x1)
    h2 = (n2 * small_ref[2:3] + small_ref[3:4]).astype(BF16)
    return n1, r1, h, o, x1, n2, r2, h2


def gelu_parts(u):
    cdf = 0.5 * (1.0 + lax.erf(u * np.float32(0.5**0.5)))
    return cdf


def fwd_kernel(x_ref, small_ref, fc1b_ref, wqkv_ref, wproj_ref, wfc1_ref, wfc2_ref, bias_ref,
               y_ref, qkv_s, o_s):
    def one_image(img, carry):
        x = x_ref[img].astype(F32)
        parts = forward_half(x, small_ref, wqkv_ref, wproj_ref, bias_ref, qkv_s, o_s, None)
        x1, h2 = parts[4], parts[7]
        total = x1 + small_ref[7:8]
        for c in range(FF // 512):
            cols = slice(c * 512, (c + 1) * 512)
            u = dot(h2, wfc1_ref[:, cols], 1, 0) + fc1b_ref[0:1, cols]
            a = (u * gelu_parts(u)).astype(BF16)
            total = total + dot(a, wfc2_ref[:, cols], 1, 1)
        y_ref[img] = total.astype(BF16)
        return carry

    lax.fori_loop(0, x_ref.shape[0], one_image, 0)


def bwd_kernel(x_ref, g_ref, small_ref, fc1b_ref, wqkv_ref, wproj_ref, wfc1_ref, wfc2_ref, bias_ref,
               dx_ref, gqkv_ref, gproj_ref, gfc1_ref, gfc2_ref, gsmall_ref, gfc1b_ref, gtable_ref,
               qkv_s, o_s, p_s, do_s, h_all, o_all, h2_all, dz_all, dy_all, a_all, du_all, dqkv_all):
    gsmall_ref[...] = jnp.zeros_like(gsmall_ref)
    gfc1b_ref[...] = jnp.zeros_like(gfc1b_ref)
    gtable_ref[...] = jnp.zeros_like(gtable_ref)

    def add_row(row, values):
        gsmall_ref[row : row + 1] += jnp.sum(values, axis=0, keepdims=True)

    def one_image(img, carry):
        base = pl.multiple_of(img * IMG_ROWS, IMG_ROWS)
        rows = pl.ds(base, IMG_ROWS)
        x = x_ref[img].astype(F32)
        n1, r1, h, o, x1, n2, r2, h2 = forward_half(
            x, small_ref, wqkv_ref, wproj_ref, bias_ref, qkv_s, o_s, p_s
        )
        h_all[rows] = h
        o_all[rows] = o
        h2_all[rows] = h2
        dz = g_ref[img]
        dz_all[rows] = dz
        g_out = dz.astype(F32)
        add_row(7, g_out)
        dh2 = jnp.zeros((IMG_ROWS, D), F32)
        for c in range(FF // 512):
            cols = slice(c * 512, (c + 1) * 512)
            u = dot(h2, wfc1_ref[:, cols], 1, 0) + fc1b_ref[0:1, cols]
            cdf = gelu_parts(u)
            a_all[rows, cols] = (u * cdf).astype(BF16)
            pdf = jnp.exp(-0.5 * u * u) * np.float32((2.0 * np.pi) ** -0.5)
            du = ((cdf + u * pdf) * dot(dz, wfc2_ref[:, cols], 1, 0)).astype(BF16)
            du_all[rows, cols] = du
            gfc1b_ref[0:1, cols] += jnp.sum(du.astype(F32), axis=0, keepdims=True)
            dh2 = dh2 + dot(du, wfc1_ref[:, cols], 1, 1)
        add_row(2, dh2 * n2)
        add_row(3, dh2)
        dx1 = g_out + norm_back(dh2, n2, r2, small_ref[2:3])
        dy = dx1.astype(BF16)
        dy_all[rows] = dy
        add_row(6, dy.astype(F32))
        do_s[...] = dot(dy, wproj_ref[...], 1, 0).astype(BF16)
        attend_back(qkv_s, do_s, p_s, dqkv_all, base, gtable_ref)
        dq = dqkv_all[rows, 0:D]
        dk = dqkv_all[rows, D : 2 * D]
        dv = dqkv_all[rows, 2 * D : 3 * D]
        add_row(4, dq.astype(F32))
        add_row(5, dv.astype(F32))
        dh = dot(dq, wqkv_ref[0], 1, 1) + dot(dk, wqkv_ref[1], 1, 1) + dot(dv, wqkv_ref[2], 1, 1)
        add_row(0, dh * n1)
        add_row(1, dh)
        dx_ref[img] = (dx1 + norm_back(dh, n1, r1, small_ref[0:1])).astype(BF16)
        return carry

    lax.fori_loop(0, x_ref.shape[0], one_image, 0)
    for c in range(3):
        gqkv_ref[c] = dot(h_all[...], dqkv_all[:, c * D : (c + 1) * D], 0, 0).astype(BF16)
    gproj_ref[...] = dot(dy_all[...], o_all[...], 0, 0).astype(BF16)
    for c in range(FF // 512):
        cols = slice(c * 512, (c + 1) * 512)
        gfc1_ref[:, cols] = dot(h2_all[...], du_all[:, cols], 0, 0).astype(BF16)
        gfc2_ref[:, cols] = dot(dz_all[...], a_all[:, cols], 0, 0).astype(BF16)


VMEM = pl.BlockSpec(memory_space=pltpu.VMEM)


def layer_cost(images, passes):
    tokens = images * IMG_ROWS
    return pl.CostEstimate(
        flops=passes * tokens * 2 * (4 * D * D + 2 * D * FF),
        bytes_accessed=20_000_000,
        transcendentals=tokens * (FF + HEADS * WP),
    )


def run_forward(x, small, fc1b, mats, bias):
    images = x.shape[0]
    return pl.pallas_call(
        fwd_kernel,
        out_shape=jax.ShapeDtypeStruct(x.shape, BF16),
        in_specs=[VMEM] * 8,
        out_specs=VMEM,
        scratch_shapes=[pltpu.VMEM((IMG_ROWS, 3 * D), BF16), pltpu.VMEM((IMG_ROWS, D), BF16)],
        compiler_params=pltpu.CompilerParams(vmem_limit_bytes=40 * 1024 * 1024),
        cost_estimate=layer_cost(images, 3),
    )(x, small, fc1b, *mats, bias)


def run_backward(x, grad, small, fc1b, mats, bias):
    images = x.shape[0]
    tokens = images * IMG_ROWS
    shape = jax.ShapeDtypeStruct
    return pl.pallas_call(
        bwd_kernel,
        out_shape=[
            shape(x.shape, BF16),
            shape((3, D, D), BF16),
            shape((D, D), BF16),
            shape((D, FF), BF16),
            shape((D, FF), BF16),
            shape((8, D), F32),
            shape((1, FF), F32),
            shape((NG, WP, GH * WP), F32),
        ],
        in_specs=[VMEM] * 9,
        out_specs=[VMEM] * 8,
        scratch_shapes=[
            pltpu.VMEM((IMG_ROWS, 3 * D), BF16),
            pltpu.VMEM((IMG_ROWS, D), BF16),
            pltpu.VMEM((NW, NG, WP, GH * WP), F32),
            pltpu.VMEM((IMG_ROWS, D), BF16),
            pltpu.VMEM((tokens, D), BF16),
            pltpu.VMEM((tokens, D), BF16),
            pltpu.VMEM((tokens, D), BF16),
            pltpu.VMEM((tokens, D), BF16),
            pltpu.VMEM((tokens, D), BF16),
            pltpu.VMEM((tokens, FF), BF16),
            pltpu.VMEM((tokens, FF), BF16),
            pltpu.VMEM((tokens, 3 * D), BF16),
        ],
        compiler_params=pltpu.CompilerParams(vmem_limit_bytes=56 * 1024 * 1024),
        cost_estimate=layer_cost(images, 9),
    )(x, grad, small, fc1b, *mats, bias)


def pack_shard(qkv, proj, fc1, fc2):
    rows, cols = proj.shape
    def quarters(m):
        return m.reshape(rows, FF // D, cols).transpose(1, 0, 2).reshape(-1, cols)
    return jnp.concatenate([qkv.reshape(-1, cols), proj, quarters(fc1), quarters(fc2)], axis=0)


def unpack_shard(packed, rows, cols):
    def wide(m):
        return m.reshape(FF // D, rows, cols).transpose(1, 0, 2).reshape(rows, FF // D * cols)
    return (
        packed[: 3 * rows].reshape(3, rows, cols),
        packed[3 * rows : 4 * rows],
        wide(packed[4 * rows : 8 * rows]),
        wide(packed[8 * rows :]),
    )


def unpack_full(gathered, dp, tensor, rows, cols):
    parts = gathered.reshape(dp, tensor, 12, rows, cols)
    qkv = parts[:, :, 0:3].transpose(2, 0, 3, 1, 4).reshape(3, D, D)
    proj = parts[:, :, 3].transpose(0, 2, 1, 3).reshape(D, D)
    fc1 = parts[:, :, 4:8].transpose(0, 3, 1, 2, 4).reshape(D, FF)
    fc2 = parts[:, :, 8:12].transpose(0, 3, 1, 2, 4).reshape(D, FF)
    return qkv, proj, fc1, fc2


def pack_full(qkv, proj, fc1, fc2, dp, tensor, rows, cols):
    q = qkv.reshape(3, dp, rows, tensor, cols).transpose(1, 3, 0, 2, 4)
    p = proj.reshape(1, dp, rows, tensor, cols).transpose(1, 3, 0, 2, 4)
    f1 = fc1.reshape(dp, rows, tensor, FF // D, cols).transpose(0, 2, 3, 1, 4)
    f2 = fc2.reshape(dp, rows, tensor, FF // D, cols).transpose(0, 2, 3, 1, 4)
    return jnp.concatenate([q, p, f1, f2], axis=2).reshape(-1, cols)


def swapped(array, axis):
    return lax.ppermute(array, axis, [(0, 1), (1, 0)])


def half_of(array, which, axis):
    size = array.shape[axis] // 2
    return lax.dynamic_slice_in_dim(array, which * size, size, axis)


def on_device(ends, image_counts, norm_gains, norm_shifts, w_qkv, qv_bias, rel_table, w_proj,
              out_biases, w_fc1, fc1_bias, w_fc2):
    pipe = lax.axis_index("pipe")
    tensor = lax.axis_index("tensor")
    first = pipe == 0
    dp_n, tensor_n = lax.axis_size("dp"), lax.axis_size("tensor")
    rows, cols = w_proj.shape[1], w_proj.shape[2]

    shard = pack_shard(w_qkv[0], w_proj[0], w_fc1[0], w_fc2[0])
    kept = half_of(shard, pipe, 0)
    got = swapped(half_of(shard, 1 - pipe, 0), "pipe")
    gathered = [
        lax.all_gather(jnp.where(first, kept, got), ALL_AXES, axis=0, tiled=True),
        lax.all_gather(jnp.where(first, got, kept), ALL_AXES, axis=0, tiled=True),
    ]
    mats = [unpack_full(g, dp_n, tensor_n, rows, cols) for g in gathered]

    heads_here = rel_table.shape[1]
    sizes = (2 * D, 2 * D, 2 * D, 2 * cols, fc1_bias.shape[1], heads_here * TABLE)
    small_local = jnp.concatenate(
        [a.reshape(-1) for a in (norm_gains, norm_shifts, out_biases, qv_bias, fc1_bias, rel_table)]
    )
    small_all = lax.all_gather(small_local, ("pipe", "tensor"), axis=0, tiled=True).reshape(2, 2, -1)
    cuts = np.cumsum((0,) + sizes)
    smalls, hidden, biases = [], [], []
    region = region_masks()
    for layer in range(2):
        mine = [small_all[layer, :, cuts[i] : cuts[i + 1]] for i in range(6)]
        gains = mine[0][0].reshape(2, D)
        shifts = mine[1][0].reshape(2, D)
        outs = mine[2][0].reshape(2, D)
        qv = mine[3].reshape(2, 2, cols).transpose(1, 0, 2).reshape(2, D)
        smalls.append(
            jnp.concatenate(
                [gains[0:1], shifts[0:1], gains[1:2], shifts[1:2], qv[0:1], qv[1:2], outs], axis=0
            )
        )
        hidden.append(mine[4].reshape(1, FF))
        table = mine[5].reshape(HEADS, TABLE)
        biases.append(score_bias(table, region if layer == 1 else region[:1] * 0.0))

    own = ends[0]
    got_rows = swapped(half_of(own, 1 - pipe, 1), "pipe")
    kept_rows = half_of(own, pipe, 1)
    both = jnp.stack([jnp.where(first, kept_rows, got_rows), jnp.where(first, got_rows, kept_rows)])

    def whole_images(part):
        mine = half_of(part, tensor, 1)
        other = swapped(half_of(part, 1 - tensor, 1), "tensor")
        return jnp.concatenate(
            [jnp.where(tensor == 0, mine, other), jnp.where(tensor == 0, other, mine)], axis=0
        )

    x_tokens, c_tokens = whole_images(both[0]), whole_images(both[1])
    images = x_tokens.shape[1]
    slots = (pipe * 2 + tensor) * images + jnp.arange(images, dtype=jnp.int32)
    real = (slots < image_counts[0]).astype(BF16)
    c_tokens = c_tokens * real[None, :, None]
    order = [one_hot_order(0), one_hot_order(SHIFT)]

    def placed(matrix, tokens, spec):
        return jnp.einsum(spec, jnp.asarray(matrix, BF16), tokens, preferred_element_type=F32).astype(BF16)

    x_in = placed(order[0], x_tokens, "rs,sbd->brd")
    c_in = placed(order[1], c_tokens, "rs,sbd->brd")

    y0 = run_forward(x_in, smalls[0], hidden[0], mats[0], biases[0])
    y0 = placed(order[1] @ order[0].T, y0, "rs,bsd->brd")
    back1 = run_backward(y0, c_in, smalls[1], hidden[1], mats[1], biases[1])
    g_mid = placed(order[0] @ order[1].T, back1[0], "rs,bsd->brd")
    g1 = lax.psum_scatter(
        pack_full(*back1[1:5], dp_n, tensor_n, rows, cols), ALL_AXES, scatter_dimension=0, tiled=True
    )
    back0 = run_backward(x_in, g_mid, smalls[0], hidden[0], mats[0], biases[0])
    g0 = lax.psum_scatter(
        pack_full(*back0[1:5], dp_n, tensor_n, rows, cols), ALL_AXES, scatter_dimension=0, tiled=True
    )

    other = swapped(jnp.where(first, g1, g0), "pipe")
    mine = jnp.where(first, g0, g1)
    mats_grad = jnp.where(
        first, jnp.concatenate([mine, other], axis=0), jnp.concatenate([other, mine], axis=0)
    ).astype(F32)
    qkv_g, proj_g, fc1_g, fc2_g = unpack_shard(mats_grad, rows, cols)

    hot = rel_one_hot().reshape(TABLE, WP * WP)

    def small_grads(back):
        scores = back[7].reshape(NG, WP, GH, WP).transpose(0, 2, 1, 3).reshape(HEADS, WP * WP)
        table = lax.dot_general(scores, hot, (((1,), (1,)), ((), ())), precision=HIGHEST)
        return jnp.concatenate([back[5].reshape(-1), back[6].reshape(-1), table.reshape(-1)])

    summed = lax.psum(jnp.stack([small_grads(back0), small_grads(back1)]), ALL_AXES)
    summed = jnp.where(first, summed[0], summed[1])
    rows_g = summed[: 8 * D].reshape(8, D)
    gains_g = jnp.stack([rows_g[0], rows_g[2]])
    shifts_g = jnp.stack([rows_g[1], rows_g[3]])
    qv_g = half_of(rows_g[4:6], tensor, 1)
    outs_g = rows_g[6:8]
    fc1b_g = half_of(summed[8 * D : 8 * D + FF], tensor, 0)
    table_g = half_of(summed[8 * D + FF :].reshape(HEADS, TABLE), tensor, 0)

    dx = placed(order[0], back0[0], "rs,brd->sbd")
    gm = placed(order[0], g_mid, "rs,brd->sbd")

    def split_rows(tokens):
        mine = half_of(tokens, tensor, 0)
        other = swapped(half_of(tokens, 1 - tensor, 0), "tensor")
        return jnp.concatenate(
            [jnp.where(tensor == 0, mine, other), jnp.where(tensor == 0, other, mine)], axis=1
        )

    dx, gm = split_rows(dx), split_rows(gm)
    other = swapped(jnp.where(first, gm, dx), "pipe")
    mine = jnp.where(first, dx, gm)
    section = jnp.where(
        first, jnp.concatenate([mine, other], axis=1), jnp.concatenate([other, mine], axis=1)
    )
    return (
        section[None],
        gains_g[None],
        shifts_g[None],
        qkv_g[None],
        qv_g[None],
        table_g[None],
        proj_g[None],
        outs_g[None],
        fc1_g[None],
        fc1b_g[None],
        fc2_g[None],
    )


def solution(mesh):
    return jax.shard_map(
        on_device,
        mesh=mesh,
        in_specs=(
            P("pipe", "tensor", "dp", None),
            P("dp"),
            P("pipe", None, None),
            P("pipe", None, None),
            P("pipe", None, "dp", "tensor"),
            P("pipe", None, "tensor"),
            P("pipe", "tensor", None),
            P("pipe", "dp", "tensor"),
            P("pipe", None, None),
            P("pipe", "dp", "tensor"),
            P("pipe", "tensor"),
            P("pipe", "dp", "tensor"),
        ),
        out_specs=(
            P("pipe", "tensor", "dp", None),
            P("pipe", None, None),
            P("pipe", None, None),
            P("pipe", None, "dp", "tensor"),
            P("pipe", None, "tensor"),
            P("pipe", "tensor", None),
            P("pipe", "dp", "tensor"),
            P("pipe", None, None),
            P("pipe", "dp", "tensor"),
            P("pipe", "tensor"),
            P("pipe", "dp", "tensor"),
        ),
        check_vma=False,
    )
```

```python
from functools import partial

import jax
import jax.numpy as jnp
import numpy as np
from jax import lax
from jax.experimental import pallas as pl
from jax.experimental.pallas import tpu as pltpu
from jax.sharding import PartitionSpec as P

D = 512
HEADS = 16
HD = 32
FF = 2048
SIDE = 14
WIN = 7
SHIFT = 3
NW = 4
WP = 64
IMG_ROWS = NW * WP
GH = 4
NG = HEADS // GH
Q_SCALE = HD ** (-0.5)
TABLE = (2 * WIN - 1) ** 2
F32 = jnp.float32
BF16 = jnp.bfloat16
HIGHEST = lax.Precision.HIGHEST
ALL_AXES = ("dp", "tensor", "pipe")


def token_order(offset):
    order = np.full((IMG_ROWS,), -1, np.int64)
    per_side = SIDE // WIN
    for win in range(NW):
        for place in range(WIN * WIN):
            row = (win // per_side) * WIN + place // WIN
            col = (win % per_side) * WIN + place % WIN
            order[win * WP + place] = ((row + offset) % SIDE) * SIDE + (col + offset) % SIDE
    return order


def one_hot_order(offset):
    order = token_order(offset)
    return (order[:, None] == np.arange(SIDE * SIDE)[None, :]).astype(np.float32)


def rel_one_hot():
    places = np.arange(WP)
    rows_in, cols_in = places // WIN, places % WIN
    index = (rows_in[None, :] - rows_in[:, None] + WIN - 1) * (2 * WIN - 1) + (
        cols_in[None, :] - cols_in[:, None] + WIN - 1
    )
    real = places < WIN * WIN
    index = np.where(real[:, None] & real[None, :], index, -1).astype(np.int32)
    return (jnp.asarray(index)[None] == jnp.arange(TABLE, dtype=jnp.int32)[:, None, None]).astype(F32)


def region_masks():
    def region(pos):
        return (pos >= SIDE - WIN).astype(np.int64) + (pos >= SIDE - SHIFT).astype(np.int64)

    per_side = SIDE // WIN
    out = np.zeros((NW, WP, WP), np.float32)
    places = np.arange(WIN * WIN)
    for win in range(NW):
        row = (win // per_side) * WIN + places // WIN
        col = (win % per_side) * WIN + places % WIN
        label = 3 * region(row) + region(col)
        out[win, : WIN * WIN, : WIN * WIN] = np.where(label[:, None] != label[None, :], -100.0, 0.0)
    return out


def score_bias(table, mask):
    hot = rel_one_hot().reshape(TABLE, WP * WP)
    bias = jnp.dot(table, hot, precision=HIGHEST).reshape(NG, GH, WP, WP)
    pad = jnp.where(jnp.arange(WP) >= WIN * WIN, -1e30, 0.0).astype(F32)
    bias = bias.transpose(0, 2, 1, 3)[None] + pad[None, None, :, None, None]
    bias = bias + jnp.asarray(mask)[:, None, :, None, :]
    return bias.reshape(mask.shape[0], NG, WP, GH * WP)


def dot(a, b, a_dim, b_dim):
    return lax.dot_general(a, b, (((a_dim,), (b_dim,)), ((), ())), preferred_element_type=F32)


def normalize(values):
    center = values - jnp.mean(values, axis=-1, keepdims=True)
    spread = jnp.mean(center * center, axis=-1, keepdims=True)
    rstd = lax.rsqrt(spread + 1e-05)
    return center * rstd, rstd


def norm_back(grad, n, rstd, gain):
    e = grad * gain
    return rstd * (
        e - jnp.mean(e, axis=-1, keepdims=True) - n * jnp.mean(e * n, axis=-1, keepdims=True)
    )


def spread_heads(block):
    lane_head = lax.broadcasted_iota(jnp.int32, block.shape, 1) // HD
    wide = block.astype(F32)
    return jnp.concatenate(
        [jnp.where(lane_head == h, wide, 0.0).astype(BF16) for h in range(GH)], axis=0
    )


def fold_heads(block):
    lane_head = lax.broadcasted_iota(jnp.int32, (WP, GH * HD), 1) // HD
    out = jnp.zeros((WP, GH * HD), F32)
    for h in range(GH):
        out = jnp.where(lane_head == h, block[h * WP : (h + 1) * WP], out)
    return out


def softmax_rows(scores):
    top = jnp.max(scores, axis=0, keepdims=True)
    part = jnp.exp(scores - top)
    return part / jnp.sum(part, axis=0, keepdims=True)


def attend(bias_ref, qkv_s, o_s, p_s):
    wins = bias_ref.shape[0]

    def one_window(win, carry):
        rows = pl.ds(pl.multiple_of(win * WP, WP), WP)
        for g in range(NG):
            lanes = slice(g * 128, (g + 1) * 128)
            q = qkv_s[rows, lanes]
            k = qkv_s[rows, D + g * 128 : D + (g + 1) * 128]
            v = qkv_s[rows, 2 * D + g * 128 : 2 * D + (g + 1) * 128]
            bias = bias_ref[win, g] if wins > 1 else bias_ref[0, g]
            p = softmax_rows(dot(k, spread_heads(q), 1, 1) + bias)
            if p_s is not None:
                p_s[win, g] = p
            o_s[rows, lanes] = fold_heads(dot(p.astype(BF16), v, 0, 0)).astype(BF16)
        return carry

    lax.fori_loop(0, NW, one_window, 0)


def attend_back(qkv_s, do_s, p_s, dqkv_ref, base, table_ref):
    def one_window(win, carry):
        rows = pl.ds(pl.multiple_of(win * WP, WP), WP)
        out_rows = pl.ds(pl.multiple_of(base + win * WP, WP), WP)
        for g in range(NG):
            lanes = slice(g * 128, (g + 1) * 128)
            k_lanes = slice(D + g * 128, D + (g + 1) * 128)
            v_lanes = slice(2 * D + g * 128, 2 * D + (g + 1) * 128)
            q_wide = spread_heads(qkv_s[rows, lanes])
            do_wide = spread_heads(do_s[rows, lanes])
            k = qkv_s[rows, k_lanes]
            v = qkv_s[rows, v_lanes]
            p = p_s[win, g]
            dp = dot(v, do_wide, 1, 1)
            ds = (p * (dp - jnp.sum(p * dp, axis=0, keepdims=True))).astype(BF16)
            table_ref[g] += ds.astype(F32)
            dqkv_ref[out_rows, lanes] = (fold_heads(dot(ds, k, 0, 0)) * Q_SCALE).astype(BF16)
            dqkv_ref[out_rows, k_lanes] = dot(ds, q_wide, 1, 0).astype(BF16)
            dqkv_ref[out_rows, v_lanes] = dot(p.astype(BF16), do_wide, 1, 0).astype(BF16)
        return carry

    lax.fori_loop(0, NW, one_window, 0)


def forward_half(x, small_ref, wqkv_ref, wproj_ref, bias_ref, qkv_s, o_s, p_s):
    n1, r1 = normalize(x)
    h = (n1 * small_ref[0:1] + small_ref[1:2]).astype(BF16)
    qkv_s[:, 0:D] = ((dot(h, wqkv_ref[0], 1, 0) + small_ref[4:5]) * Q_SCALE).astype(BF16)
    qkv_s[:, D : 2 * D] = dot(h, wqkv_ref[1], 1, 0).astype(BF16)
    qkv_s[:, 2 * D : 3 * D] = (dot(h, wqkv_ref[2], 1, 0) + small_ref[5:6]).astype(BF16)
    attend(bias_ref, qkv_s, o_s, p_s)
    o = o_s[...]
    x1 = x + (dot(o, wproj_ref[...], 1, 1) + small_ref[6:7])
    n2, r2 = normalize(x1)
    h2 = (n2 * small_ref[2:3] + small_ref[3:4]).astype(BF16)
    return n1, r1, h, o, x1, n2, r2, h2


def gelu_parts(u):
    cdf = 0.5 * (1.0 + lax.erf(u * np.float32(0.5**0.5)))
    return cdf


CHUNK = 64
COLS = 256
BLOCKS = D // CHUNK


def packed_places():
    places = [(c, c, 0) for c in range(3)] + [(3, 3, 0)]
    places += [(4 + n, 4, n * COLS) for n in range(FF // D)]
    places += [(8 + n, 5, n * COLS) for n in range(FF // D)]
    return places


def unpack_weights(packed_ref, wqkv_s, wproj_s, wfc1_s, wfc2_s):
    targets = [wqkv_s.at[0], wqkv_s.at[1], wqkv_s.at[2], wproj_s, wfc1_s, wfc2_s]
    for piece, which, col in packed_places():
        width = targets[which].shape[1] // 2
        for half in range(2):
            lanes = slice(half * width + col, half * width + col + COLS)
            for block in range(BLOCKS):
                targets[which][block * CHUNK : (block + 1) * CHUNK, lanes] = packed_ref[
                    block, half, piece * CHUNK : (piece + 1) * CHUNK, :
                ]


def store_packed(packed_ref, piece, half, values):
    for block in range(BLOCKS):
        packed_ref[half, block, piece * CHUNK : (piece + 1) * CHUNK, :] = values[
            block * CHUNK : (block + 1) * CHUNK
        ]


def fwd_kernel(x_ref, small_ref, fc1b_ref, packed_ref, bias_ref,
               y_ref, qkv_s, o_s, wqkv_ref, wproj_ref, wfc1_ref, wfc2_ref):
    unpack_weights(packed_ref, wqkv_ref, wproj_ref, wfc1_ref, wfc2_ref)

    def one_image(img, carry):
        x = x_ref[img].astype(F32)
        parts = forward_half(x, small_ref, wqkv_ref, wproj_ref, bias_ref, qkv_s, o_s, None)
        x1, h2 = parts[4], parts[7]
        total = x1 + small_ref[7:8]
        for c in range(FF // 512):
            cols = slice(c * 512, (c + 1) * 512)
            u = dot(h2, wfc1_ref[:, cols], 1, 0) + fc1b_ref[0:1, cols]
            a = (u * gelu_parts(u)).astype(BF16)
            total = total + dot(a, wfc2_ref[:, cols], 1, 1)
        y_ref[img] = total.astype(BF16)
        return carry

    lax.fori_loop(0, x_ref.shape[0], one_image, 0)


def bwd_kernel(x_ref, g_ref, small_ref, fc1b_ref, packed_ref, bias_ref,
               dx_ref, gmats_ref, gsmall_ref, gfc1b_ref, gtable_ref,
               qkv_s, o_s, p_s, do_s, h_all, o_all, h2_all, dz_all, dy_all, a_all, du_all, dqkv_all,
               wqkv_ref, wproj_ref, wfc1_ref, wfc2_ref):
    unpack_weights(packed_ref, wqkv_ref, wproj_ref, wfc1_ref, wfc2_ref)
    gsmall_ref[...] = jnp.zeros_like(gsmall_ref)
    gfc1b_ref[...] = jnp.zeros_like(gfc1b_ref)
    gtable_ref[...] = jnp.zeros_like(gtable_ref)

    def add_row(row, values):
        gsmall_ref[row : row + 1] += jnp.sum(values, axis=0, keepdims=True)

    def one_image(img, carry):
        base = pl.multiple_of(img * IMG_ROWS, IMG_ROWS)
        rows = pl.ds(base, IMG_ROWS)
        x = x_ref[img].astype(F32)
        n1, r1, h, o, x1, n2, r2, h2 = forward_half(
            x, small_ref, wqkv_ref, wproj_ref, bias_ref, qkv_s, o_s, p_s
        )
        h_all[rows] = h
        o_all[rows] = o
        h2_all[rows] = h2
        dz = g_ref[img]
        dz_all[rows] = dz
        g_out = dz.astype(F32)
        add_row(7, g_out)
        dh2 = jnp.zeros((IMG_ROWS, D), F32)
        for c in range(FF // 512):
            cols = slice(c * 512, (c + 1) * 512)
            u = dot(h2, wfc1_ref[:, cols], 1, 0) + fc1b_ref[0:1, cols]
            cdf = gelu_parts(u)
            a_all[rows, cols] = (u * cdf).astype(BF16)
            pdf = jnp.exp(-0.5 * u * u) * np.float32((2.0 * np.pi) ** -0.5)
            du = ((cdf + u * pdf) * dot(dz, wfc2_ref[:, cols], 1, 0)).astype(BF16)
            du_all[rows, cols] = du
            gfc1b_ref[0:1, cols] += jnp.sum(du.astype(F32), axis=0, keepdims=True)
            dh2 = dh2 + dot(du, wfc1_ref[:, cols], 1, 1)
        add_row(2, dh2 * n2)
        add_row(3, dh2)
        dx1 = g_out + norm_back(dh2, n2, r2, small_ref[2:3])
        dy = dx1.astype(BF16)
        dy_all[rows] = dy
        add_row(6, dy.astype(F32))
        do_s[...] = dot(dy, wproj_ref[...], 1, 0).astype(BF16)
        attend_back(qkv_s, do_s, p_s, dqkv_all, base, gtable_ref)
        dq = dqkv_all[rows, 0:D]
        dk = dqkv_all[rows, D : 2 * D]
        dv = dqkv_all[rows, 2 * D : 3 * D]
        add_row(4, dq.astype(F32))
        add_row(5, dv.astype(F32))
        dh = dot(dq, wqkv_ref[0], 1, 1) + dot(dk, wqkv_ref[1], 1, 1) + dot(dv, wqkv_ref[2], 1, 1)
        add_row(0, dh * n1)
        add_row(1, dh)
        dx_ref[img] = (dx1 + norm_back(dh, n1, r1, small_ref[0:1])).astype(BF16)
        return carry

    lax.fori_loop(0, x_ref.shape[0], one_image, 0)
    for piece, which, col in packed_places():
        for half in range(2):
            if which < 3:
                left, right = h_all[...], dqkv_all[:, pl.ds(which * D + half * COLS, COLS)]
            elif which == 3:
                left, right = dy_all[...], o_all[:, pl.ds(half * COLS, COLS)]
            elif which == 4:
                left, right = h2_all[...], du_all[:, pl.ds(half * (FF // 2) + col, COLS)]
            else:
                left, right = dz_all[...], a_all[:, pl.ds(half * (FF // 2) + col, COLS)]
            store_packed(gmats_ref, piece, half, dot(left, right, 0, 0).astype(BF16))


VMEM = pl.BlockSpec(memory_space=pltpu.VMEM)


def layer_cost(images, passes):
    tokens = images * IMG_ROWS
    return pl.CostEstimate(
        flops=passes * tokens * 2 * (4 * D * D + 2 * D * FF),
        bytes_accessed=20_000_000,
        transcendentals=tokens * (FF + HEADS * WP),
    )


def run_forward(x, small, fc1b, mats, bias):
    images = x.shape[0]
    return pl.pallas_call(
        fwd_kernel,
        out_shape=jax.ShapeDtypeStruct(x.shape, BF16),
        in_specs=[VMEM] * 5,
        out_specs=VMEM,
        scratch_shapes=[
            pltpu.VMEM((IMG_ROWS, 3 * D), BF16),
            pltpu.VMEM((IMG_ROWS, D), BF16),
            pltpu.VMEM((3, D, D), BF16),
            pltpu.VMEM((D, D), BF16),
            pltpu.VMEM((D, FF), BF16),
            pltpu.VMEM((D, FF), BF16),
        ],
        compiler_params=pltpu.CompilerParams(vmem_limit_bytes=40 * 1024 * 1024),
        cost_estimate=layer_cost(images, 3),
    )(x, small, fc1b, mats, bias)


def run_backward(x, grad, small, fc1b, mats, bias):
    images = x.shape[0]
    tokens = images * IMG_ROWS
    shape = jax.ShapeDtypeStruct
    return pl.pallas_call(
        bwd_kernel,
        out_shape=[
            shape(x.shape, BF16),
            shape((2, BLOCKS, 12 * CHUNK, COLS), BF16),
            shape((8, D), F32),
            shape((1, FF), F32),
            shape((NG, WP, GH * WP), F32),
        ],
        in_specs=[VMEM] * 6,
        out_specs=[VMEM] * 5,
        scratch_shapes=[
            pltpu.VMEM((IMG_ROWS, 3 * D), BF16),
            pltpu.VMEM((IMG_ROWS, D), BF16),
            pltpu.VMEM((NW, NG, WP, GH * WP), F32),
            pltpu.VMEM((IMG_ROWS, D), BF16),
            pltpu.VMEM((tokens, D), BF16),
            pltpu.VMEM((tokens, D), BF16),
            pltpu.VMEM((tokens, D), BF16),
            pltpu.VMEM((tokens, D), BF16),
            pltpu.VMEM((tokens, D), BF16),
            pltpu.VMEM((tokens, FF), BF16),
            pltpu.VMEM((tokens, FF), BF16),
            pltpu.VMEM((tokens, 3 * D), BF16),
            pltpu.VMEM((3, D, D), BF16),
            pltpu.VMEM((D, D), BF16),
            pltpu.VMEM((D, FF), BF16),
            pltpu.VMEM((D, FF), BF16),
        ],
        compiler_params=pltpu.CompilerParams(vmem_limit_bytes=56 * 1024 * 1024),
        cost_estimate=layer_cost(images, 9),
    )(x, grad, small, fc1b, mats, bias)


def pack_shard(qkv, proj, fc1, fc2):
    rows, cols = proj.shape
    def quarters(m):
        return m.reshape(rows, FF // D, cols).transpose(1, 0, 2).reshape(-1, cols)
    return jnp.concatenate([qkv.reshape(-1, cols), proj, quarters(fc1), quarters(fc2)], axis=0)


def unpack_shard(packed, rows, cols):
    def wide(m):
        return m.reshape(FF // D, rows, cols).transpose(1, 0, 2).reshape(rows, FF // D * cols)
    return (
        packed[: 3 * rows].reshape(3, rows, cols),
        packed[3 * rows : 4 * rows],
        wide(packed[4 * rows : 8 * rows]),
        wide(packed[8 * rows :]),
    )


def to_blocks(gathered, dp, rows):
    parts = gathered.reshape(BLOCKS, dp // BLOCKS, 2, 12, rows, COLS)
    return parts.transpose(0, 2, 3, 1, 4, 5).reshape(BLOCKS, 2, 12 * CHUNK, COLS)


def from_blocks(blocks, dp, rows):
    parts = blocks.reshape(2, BLOCKS, 12, dp // BLOCKS, rows, COLS)
    return parts.transpose(0, 1, 3, 2, 4, 5).reshape(2, dp, 12 * rows, COLS)


def exchange_half(array, axis, name, bit):
    bits = [(i, i ^ (1 << bit)) for i in range(lax.axis_size(name))]
    which = (lax.axis_index(name) >> bit) & 1
    there = lax.ppermute(half_of(array, 1 - which, axis), name, bits)
    return (half_of(array, which, axis).astype(F32) + there.astype(F32)).astype(BF16)


def total_of(array, dp):
    array = array + swapped(array, "tensor")
    array = array + swapped(array, "pipe")
    for bit in range(dp.bit_length() - 1):
        array = array + lax.ppermute(array, "dp", [(i, i ^ (1 << bit)) for i in range(dp)])
    return array


def scatter_sum(blocks, dp, rows):
    array = from_blocks(blocks, dp, rows)
    array = exchange_half(array, 0, "tensor", 0)
    levels = dp.bit_length() - 1
    array = array.reshape((2,) * levels + (2, 6 * rows, COLS))
    last = levels - 1
    done = []
    for part in range(2):
        one = array[..., part * (COLS // 2) : (part + 1) * (COLS // 2)]
        if part == 0:
            one = exchange_half(one, levels, "pipe", 0)
            one = exchange_half(one, last, "dp", 0)
        else:
            one = exchange_half(one, last, "dp", 0)
            one = exchange_half(one, levels, "pipe", 0)
        for level in range(levels - 1):
            one = exchange_half(one, level, "dp", levels - 1 - level)
        done.append(one.reshape(6 * rows, COLS // 2))
    return jnp.concatenate(done, axis=1)


def swapped(array, axis):
    return lax.ppermute(array, axis, [(0, 1), (1, 0)])


def half_of(array, which, axis):
    size = array.shape[axis] // 2
    return lax.dynamic_slice_in_dim(array, which * size, size, axis)


def on_device(ends, image_counts, norm_gains, norm_shifts, w_qkv, qv_bias, rel_table, w_proj,
              out_biases, w_fc1, fc1_bias, w_fc2):
    pipe = lax.axis_index("pipe")
    tensor = lax.axis_index("tensor")
    first = pipe == 0
    dp_n = lax.axis_size("dp")
    rows, cols = w_proj.shape[1], w_proj.shape[2]

    shard = pack_shard(w_qkv[0], w_proj[0], w_fc1[0], w_fc2[0])
    kept = half_of(shard, pipe, 0)
    got = swapped(half_of(shard, 1 - pipe, 0), "pipe")
    gathered = [
        lax.all_gather(jnp.where(first, kept, got), ALL_AXES, axis=0, tiled=True),
        lax.all_gather(jnp.where(first, got, kept), ALL_AXES, axis=0, tiled=True),
    ]
    mats = [to_blocks(gathered[0], dp_n, rows)]

    heads_here = rel_table.shape[1]
    sizes = (2 * D, 2 * D, 2 * D, 2 * cols, fc1_bias.shape[1], heads_here * TABLE)
    small_local = jnp.concatenate(
        [a.reshape(-1) for a in (norm_gains, norm_shifts, out_biases, qv_bias, fc1_bias, rel_table)]
    )
    small_all = lax.all_gather(small_local, ("pipe", "tensor"), axis=0, tiled=True).reshape(2, 2, -1)
    cuts = np.cumsum((0,) + sizes)
    smalls, hidden, biases = [], [], []
    region = region_masks()
    for layer in range(2):
        mine = [small_all[layer, :, cuts[i] : cuts[i + 1]] for i in range(6)]
        gains = mine[0][0].reshape(2, D)
        shifts = mine[1][0].reshape(2, D)
        outs = mine[2][0].reshape(2, D)
        qv = mine[3].reshape(2, 2, cols).transpose(1, 0, 2).reshape(2, D)
        smalls.append(
            jnp.concatenate(
                [gains[0:1], shifts[0:1], gains[1:2], shifts[1:2], qv[0:1], qv[1:2], outs], axis=0
            )
        )
        hidden.append(mine[4].reshape(1, FF))
        table = mine[5].reshape(HEADS, TABLE)
        biases.append(score_bias(table, region if layer == 1 else region[:1] * 0.0))

    own = ends[0]
    got_rows = swapped(half_of(own, 1 - pipe, 1), "pipe")
    kept_rows = half_of(own, pipe, 1)
    both = jnp.stack([jnp.where(first, kept_rows, got_rows), jnp.where(first, got_rows, kept_rows)])

    def whole_images(part):
        mine = half_of(part, tensor, 1)
        other = swapped(half_of(part, 1 - tensor, 1), "tensor")
        return jnp.concatenate(
            [jnp.where(tensor == 0, mine, other), jnp.where(tensor == 0, other, mine)], axis=0
        )

    x_tokens, c_tokens = whole_images(both[0]), whole_images(both[1])
    images = x_tokens.shape[1]
    slots = (pipe * 2 + tensor) * images + jnp.arange(images, dtype=jnp.int32)
    real = (slots < image_counts[0]).astype(BF16)
    c_tokens = c_tokens * real[None, :, None]
    order = [one_hot_order(0), one_hot_order(SHIFT)]

    def placed(matrix, tokens, spec):
        return jnp.einsum(spec, jnp.asarray(matrix, BF16), tokens, preferred_element_type=F32).astype(BF16)

    x_in = placed(order[0], x_tokens, "rs,sbd->brd")
    c_in = placed(order[1], c_tokens, "rs,sbd->brd")

    y0 = run_forward(x_in, smalls[0], hidden[0], mats[0], biases[0])
    y0, second_mats = lax.optimization_barrier((y0, gathered[1]))
    y0 = placed(order[1] @ order[0].T, y0, "rs,bsd->brd")
    back1 = run_backward(y0, c_in, smalls[1], hidden[1], to_blocks(second_mats, dp_n, rows), biases[1])
    g_mid = placed(order[0] @ order[1].T, back1[0], "rs,bsd->brd")
    g1 = lax.psum_scatter(
        from_blocks(back1[1], dp_n, rows).reshape(-1, cols),
        ("tensor", "dp", "pipe"),
        scatter_dimension=0,
        tiled=True,
    )
    back0 = run_backward(x_in, g_mid, smalls[0], hidden[0], mats[0], biases[0])
    g0 = scatter_sum(back0[1], dp_n, rows)

    other = swapped(jnp.where(first, g1, g0), "pipe")
    mine = jnp.where(first, g0, g1)
    mats_grad = jnp.where(
        first, jnp.concatenate([mine, other], axis=0), jnp.concatenate([other, mine], axis=0)
    ).astype(F32)
    qkv_g, proj_g, fc1_g, fc2_g = unpack_shard(mats_grad, rows, cols)

    hot = rel_one_hot().reshape(TABLE, WP * WP)

    def small_grads(back):
        scores = back[4].reshape(NG, WP, GH, WP).transpose(0, 2, 1, 3).reshape(HEADS, WP * WP)
        table = lax.dot_general(scores, hot, (((1,), (1,)), ((), ())), precision=HIGHEST)
        return jnp.concatenate([back[2].reshape(-1), back[3].reshape(-1), table.reshape(-1)])

    summed = total_of(jnp.stack([small_grads(back0), small_grads(back1)]), dp_n)
    summed = jnp.where(first, summed[0], summed[1])
    rows_g = summed[: 8 * D].reshape(8, D)
    gains_g = jnp.stack([rows_g[0], rows_g[2]])
    shifts_g = jnp.stack([rows_g[1], rows_g[3]])
    qv_g = half_of(rows_g[4:6], tensor, 1)
    outs_g = rows_g[6:8]
    fc1b_g = half_of(summed[8 * D : 8 * D + FF], tensor, 0)
    table_g = half_of(summed[8 * D + FF :].reshape(HEADS, TABLE), tensor, 0)

    dx = placed(order[0], back0[0], "rs,brd->sbd")
    gm = placed(order[0], g_mid, "rs,brd->sbd")

    def split_rows(tokens):
        mine = half_of(tokens, tensor, 0)
        other = swapped(half_of(tokens, 1 - tensor, 0), "tensor")
        return jnp.concatenate(
            [jnp.where(tensor == 0, mine, other), jnp.where(tensor == 0, other, mine)], axis=1
        )

    dx, gm = split_rows(dx), split_rows(gm)
    other = swapped(jnp.where(first, gm, dx), "pipe")
    mine = jnp.where(first, dx, gm)
    section = jnp.where(
        first, jnp.concatenate([mine, other], axis=1), jnp.concatenate([other, mine], axis=1)
    )
    return (
        section[None],
        gains_g[None],
        shifts_g[None],
        qkv_g[None],
        qv_g[None],
        table_g[None],
        proj_g[None],
        outs_g[None],
        fc1_g[None],
        fc1b_g[None],
        fc2_g[None],
    )


def solution(mesh):
    return jax.shard_map(
        on_device,
        mesh=mesh,
        in_specs=(
            P("pipe", "tensor", "dp", None),
            P("dp"),
            P("pipe", None, None),
            P("pipe", None, None),
            P("pipe", None, "dp", "tensor"),
            P("pipe", None, "tensor"),
            P("pipe", "tensor", None),
            P("pipe", "dp", "tensor"),
            P("pipe", None, None),
            P("pipe", "dp", "tensor"),
            P("pipe", "tensor"),
            P("pipe", "dp", "tensor"),
        ),
        out_specs=(
            P("pipe", "tensor", "dp", None),
            P("pipe", None, None),
            P("pipe", None, None),
            P("pipe", None, "dp", "tensor"),
            P("pipe", None, "tensor"),
            P("pipe", "tensor", None),
            P("pipe", "dp", "tensor"),
            P("pipe", None, None),
            P("pipe", "dp", "tensor"),
            P("pipe", "tensor"),
            P("pipe", "dp", "tensor"),
        ),
        check_vma=False,
    )
```

```python
from functools import partial

import jax
import jax.numpy as jnp
import numpy as np
from jax import lax
from jax.experimental import pallas as pl
from jax.experimental.pallas import tpu as pltpu
from jax.sharding import PartitionSpec as P

D = 512
HEADS = 16
HD = 32
FF = 2048
SIDE = 14
WIN = 7
SHIFT = 3
NW = 4
WP = 64
IMG_ROWS = NW * WP
GH = 4
NG = HEADS // GH
Q_SCALE = HD ** (-0.5)
TABLE = (2 * WIN - 1) ** 2
F32 = jnp.float32
BF16 = jnp.bfloat16
HIGHEST = lax.Precision.HIGHEST
ALL_AXES = ("dp", "tensor", "pipe")


def token_order(offset):
    order = np.full((IMG_ROWS,), -1, np.int64)
    per_side = SIDE // WIN
    for win in range(NW):
        for place in range(WIN * WIN):
            row = (win // per_side) * WIN + place // WIN
            col = (win % per_side) * WIN + place % WIN
            order[win * WP + place] = ((row + offset) % SIDE) * SIDE + (col + offset) % SIDE
    return order


def one_hot_order(offset):
    order = token_order(offset)
    return (order[:, None] == np.arange(SIDE * SIDE)[None, :]).astype(np.float32)


def rel_one_hot():
    places = np.arange(WP)
    rows_in, cols_in = places // WIN, places % WIN
    index = (rows_in[None, :] - rows_in[:, None] + WIN - 1) * (2 * WIN - 1) + (
        cols_in[None, :] - cols_in[:, None] + WIN - 1
    )
    real = places < WIN * WIN
    index = np.where(real[:, None] & real[None, :], index, -1).astype(np.int32)
    return (jnp.asarray(index)[None] == jnp.arange(TABLE, dtype=jnp.int32)[:, None, None]).astype(F32)


def region_masks():
    def region(pos):
        return (pos >= SIDE - WIN).astype(np.int64) + (pos >= SIDE - SHIFT).astype(np.int64)

    per_side = SIDE // WIN
    out = np.zeros((NW, WP, WP), np.float32)
    places = np.arange(WIN * WIN)
    for win in range(NW):
        row = (win // per_side) * WIN + places // WIN
        col = (win % per_side) * WIN + places % WIN
        label = 3 * region(row) + region(col)
        out[win, : WIN * WIN, : WIN * WIN] = np.where(label[:, None] != label[None, :], -100.0, 0.0)
    return out


def score_bias(table, mask):
    hot = rel_one_hot().reshape(TABLE, WP * WP)
    bias = jnp.dot(table, hot, precision=HIGHEST).reshape(NG, GH, WP, WP)
    pad = jnp.where(jnp.arange(WP) >= WIN * WIN, -1e30, 0.0).astype(F32)
    bias = bias.transpose(0, 2, 1, 3)[None] + pad[None, None, :, None, None]
    bias = bias + jnp.asarray(mask)[:, None, :, None, :]
    return bias.reshape(mask.shape[0], NG, WP, GH * WP)


def dot(a, b, a_dim, b_dim):
    return lax.dot_general(a, b, (((a_dim,), (b_dim,)), ((), ())), preferred_element_type=F32)


def normalize(values):
    center = values - jnp.mean(values, axis=-1, keepdims=True)
    spread = jnp.mean(center * center, axis=-1, keepdims=True)
    rstd = lax.rsqrt(spread + 1e-05)
    return center * rstd, rstd


def norm_back(grad, n, rstd, gain):
    e = grad * gain
    return rstd * (
        e - jnp.mean(e, axis=-1, keepdims=True) - n * jnp.mean(e * n, axis=-1, keepdims=True)
    )


def spread_heads(block):
    lane_head = lax.broadcasted_iota(jnp.int32, block.shape, 1) // HD
    wide = block.astype(F32)
    return jnp.concatenate(
        [jnp.where(lane_head == h, wide, 0.0).astype(BF16) for h in range(GH)], axis=0
    )


def fold_heads(block):
    lane_head = lax.broadcasted_iota(jnp.int32, (WP, GH * HD), 1) // HD
    out = jnp.zeros((WP, GH * HD), F32)
    for h in range(GH):
        out = jnp.where(lane_head == h, block[h * WP : (h + 1) * WP], out)
    return out


def softmax_rows(scores):
    top = jnp.max(scores, axis=0, keepdims=True)
    part = jnp.exp(scores - top)
    return part / jnp.sum(part, axis=0, keepdims=True)


def attend(bias_ref, qkv_s, o_s, p_s):
    wins = bias_ref.shape[0]

    def one_window(win, carry):
        rows = pl.ds(pl.multiple_of(win * WP, WP), WP)
        for g in range(NG):
            lanes = slice(g * 128, (g + 1) * 128)
            q = qkv_s[rows, lanes]
            k = qkv_s[rows, D + g * 128 : D + (g + 1) * 128]
            v = qkv_s[rows, 2 * D + g * 128 : 2 * D + (g + 1) * 128]
            bias = bias_ref[win, g] if wins > 1 else bias_ref[0, g]
            p = softmax_rows(dot(k, spread_heads(q), 1, 1) + bias)
            if p_s is not None:
                p_s[win, g] = p
            o_s[rows, lanes] = fold_heads(dot(p.astype(BF16), v, 0, 0)).astype(BF16)
        return carry

    lax.fori_loop(0, NW, one_window, 0)


def attend_back(qkv_s, do_s, p_s, dqkv_ref, base, table_ref):
    def one_window(win, carry):
        rows = pl.ds(pl.multiple_of(win * WP, WP), WP)
        out_rows = pl.ds(pl.multiple_of(base + win * WP, WP), WP)
        for g in range(NG):
            lanes = slice(g * 128, (g + 1) * 128)
            k_lanes = slice(D + g * 128, D + (g + 1) * 128)
            v_lanes = slice(2 * D + g * 128, 2 * D + (g + 1) * 128)
            q_wide = spread_heads(qkv_s[rows, lanes])
            do_wide = spread_heads(do_s[rows, lanes])
            k = qkv_s[rows, k_lanes]
            v = qkv_s[rows, v_lanes]
            p = p_s[win, g]
            dp = dot(v, do_wide, 1, 1)
            ds = (p * (dp - jnp.sum(p * dp, axis=0, keepdims=True))).astype(BF16)
            table_ref[g] += ds.astype(F32)
            dqkv_ref[out_rows, lanes] = (fold_heads(dot(ds, k, 0, 0)) * Q_SCALE).astype(BF16)
            dqkv_ref[out_rows, k_lanes] = dot(ds, q_wide, 1, 0).astype(BF16)
            dqkv_ref[out_rows, v_lanes] = dot(p.astype(BF16), do_wide, 1, 0).astype(BF16)
        return carry

    lax.fori_loop(0, NW, one_window, 0)


def forward_half(x, small_ref, wqkv_ref, wproj_ref, bias_ref, qkv_s, o_s, p_s):
    n1, r1 = normalize(x)
    h = (n1 * small_ref[0:1] + small_ref[1:2]).astype(BF16)
    qkv_s[:, 0:D] = ((dot(h, wqkv_ref[0], 1, 0) + small_ref[4:5]) * Q_SCALE).astype(BF16)
    qkv_s[:, D : 2 * D] = dot(h, wqkv_ref[1], 1, 0).astype(BF16)
    qkv_s[:, 2 * D : 3 * D] = (dot(h, wqkv_ref[2], 1, 0) + small_ref[5:6]).astype(BF16)
    attend(bias_ref, qkv_s, o_s, p_s)
    o = o_s[...]
    x1 = x + (dot(o, wproj_ref[...], 1, 1) + small_ref[6:7])
    n2, r2 = normalize(x1)
    h2 = (n2 * small_ref[2:3] + small_ref[3:4]).astype(BF16)
    return n1, r1, h, o, x1, n2, r2, h2


def gelu_parts(u):
    cdf = 0.5 * (1.0 + lax.erf(u * np.float32(0.5**0.5)))
    return cdf


CHUNK = 64
COLS = 256
BLOCKS = D // CHUNK


def packed_places():
    places = [(c, c, 0) for c in range(3)] + [(3, 3, 0)]
    places += [(4 + n, 4, n * COLS) for n in range(FF // D)]
    places += [(8 + n, 5, n * COLS) for n in range(FF // D)]
    return places


def unpack_weights(packed_ref, wqkv_s, wproj_s, wfc1_s, wfc2_s):
    targets = [wqkv_s.at[0], wqkv_s.at[1], wqkv_s.at[2], wproj_s, wfc1_s, wfc2_s]
    for piece, which, col in packed_places():
        width = targets[which].shape[1] // 2
        for half in range(2):
            lanes = slice(half * width + col, half * width + col + COLS)
            for block in range(BLOCKS):
                targets[which][block * CHUNK : (block + 1) * CHUNK, lanes] = packed_ref[
                    block, half, piece * CHUNK : (piece + 1) * CHUNK, :
                ]


def store_packed(packed_ref, piece, half, values):
    for block in range(BLOCKS):
        packed_ref[half, block, piece * CHUNK : (piece + 1) * CHUNK, :] = values[
            block * CHUNK : (block + 1) * CHUNK
        ]


def fwd_kernel(x_ref, small_ref, fc1b_ref, packed_ref, bias_ref,
               y_ref, qkv_s, o_s, wqkv_ref, wproj_ref, wfc1_ref, wfc2_ref):
    unpack_weights(packed_ref, wqkv_ref, wproj_ref, wfc1_ref, wfc2_ref)

    def one_image(img, carry):
        x = x_ref[img].astype(F32)
        parts = forward_half(x, small_ref, wqkv_ref, wproj_ref, bias_ref, qkv_s, o_s, None)
        x1, h2 = parts[4], parts[7]
        total = x1 + small_ref[7:8]
        for c in range(FF // 512):
            cols = slice(c * 512, (c + 1) * 512)
            u = dot(h2, wfc1_ref[:, cols], 1, 0) + fc1b_ref[0:1, cols]
            a = (u * gelu_parts(u)).astype(BF16)
            total = total + dot(a, wfc2_ref[:, cols], 1, 1)
        y_ref[img] = total.astype(BF16)
        return carry

    lax.fori_loop(0, x_ref.shape[0], one_image, 0)


def bwd_kernel(x_ref, g_ref, small_ref, fc1b_ref, packed_ref, bias_ref,
               dx_ref, gmats_ref, gsmall_ref, gfc1b_ref, gtable_ref,
               qkv_s, o_s, p_s, do_s, h_all, o_all, h2_all, dz_all, dy_all, a_all, du_all, dqkv_all,
               wqkv_ref, wproj_ref, wfc1_ref, wfc2_ref):
    unpack_weights(packed_ref, wqkv_ref, wproj_ref, wfc1_ref, wfc2_ref)
    gsmall_ref[...] = jnp.zeros_like(gsmall_ref)
    gfc1b_ref[...] = jnp.zeros_like(gfc1b_ref)
    gtable_ref[...] = jnp.zeros_like(gtable_ref)

    def add_row(row, values):
        gsmall_ref[row : row + 1] += jnp.sum(values, axis=0, keepdims=True)

    def one_image(img, carry):
        base = pl.multiple_of(img * IMG_ROWS, IMG_ROWS)
        rows = pl.ds(base, IMG_ROWS)
        x = x_ref[img].astype(F32)
        n1, r1, h, o, x1, n2, r2, h2 = forward_half(
            x, small_ref, wqkv_ref, wproj_ref, bias_ref, qkv_s, o_s, p_s
        )
        h_all[rows] = h
        o_all[rows] = o
        h2_all[rows] = h2
        dz = g_ref[img]
        dz_all[rows] = dz
        g_out = dz.astype(F32)
        add_row(7, g_out)
        dh2 = jnp.zeros((IMG_ROWS, D), F32)
        for c in range(FF // 512):
            cols = slice(c * 512, (c + 1) * 512)
            u = dot(h2, wfc1_ref[:, cols], 1, 0) + fc1b_ref[0:1, cols]
            cdf = gelu_parts(u)
            a_all[rows, cols] = (u * cdf).astype(BF16)
            pdf = jnp.exp(-0.5 * u * u) * np.float32((2.0 * np.pi) ** -0.5)
            du = ((cdf + u * pdf) * dot(dz, wfc2_ref[:, cols], 1, 0)).astype(BF16)
            du_all[rows, cols] = du
            gfc1b_ref[0:1, cols] += jnp.sum(du.astype(F32), axis=0, keepdims=True)
            dh2 = dh2 + dot(du, wfc1_ref[:, cols], 1, 1)
        add_row(2, dh2 * n2)
        add_row(3, dh2)
        dx1 = g_out + norm_back(dh2, n2, r2, small_ref[2:3])
        dy = dx1.astype(BF16)
        dy_all[rows] = dy
        add_row(6, dy.astype(F32))
        do_s[...] = dot(dy, wproj_ref[...], 1, 0).astype(BF16)
        attend_back(qkv_s, do_s, p_s, dqkv_all, base, gtable_ref)
        dq = dqkv_all[rows, 0:D]
        dk = dqkv_all[rows, D : 2 * D]
        dv = dqkv_all[rows, 2 * D : 3 * D]
        add_row(4, dq.astype(F32))
        add_row(5, dv.astype(F32))
        dh = dot(dq, wqkv_ref[0], 1, 1) + dot(dk, wqkv_ref[1], 1, 1) + dot(dv, wqkv_ref[2], 1, 1)
        add_row(0, dh * n1)
        add_row(1, dh)
        dx_ref[img] = (dx1 + norm_back(dh, n1, r1, small_ref[0:1])).astype(BF16)
        return carry

    lax.fori_loop(0, x_ref.shape[0], one_image, 0)
    for piece, which, col in packed_places():
        for half in range(2):
            if which < 3:
                left, right = h_all[...], dqkv_all[:, pl.ds(which * D + half * COLS, COLS)]
            elif which == 3:
                left, right = dy_all[...], o_all[:, pl.ds(half * COLS, COLS)]
            elif which == 4:
                left, right = h2_all[...], du_all[:, pl.ds(half * (FF // 2) + col, COLS)]
            else:
                left, right = dz_all[...], a_all[:, pl.ds(half * (FF // 2) + col, COLS)]
            store_packed(gmats_ref, piece, half, dot(left, right, 0, 0).astype(BF16))


VMEM = pl.BlockSpec(memory_space=pltpu.VMEM)


def layer_cost(images, passes):
    tokens = images * IMG_ROWS
    return pl.CostEstimate(
        flops=passes * tokens * 2 * (4 * D * D + 2 * D * FF),
        bytes_accessed=20_000_000,
        transcendentals=tokens * (FF + HEADS * WP),
    )


def run_forward(x, small, fc1b, mats, bias):
    images = x.shape[0]
    return pl.pallas_call(
        fwd_kernel,
        out_shape=jax.ShapeDtypeStruct(x.shape, BF16),
        in_specs=[VMEM] * 5,
        out_specs=VMEM,
        scratch_shapes=[
            pltpu.VMEM((IMG_ROWS, 3 * D), BF16),
            pltpu.VMEM((IMG_ROWS, D), BF16),
            pltpu.VMEM((3, D, D), BF16),
            pltpu.VMEM((D, D), BF16),
            pltpu.VMEM((D, FF), BF16),
            pltpu.VMEM((D, FF), BF16),
        ],
        compiler_params=pltpu.CompilerParams(vmem_limit_bytes=40 * 1024 * 1024),
        cost_estimate=layer_cost(images, 3),
    )(x, small, fc1b, mats, bias)


def run_backward(x, grad, small, fc1b, mats, bias):
    images = x.shape[0]
    tokens = images * IMG_ROWS
    shape = jax.ShapeDtypeStruct
    return pl.pallas_call(
        bwd_kernel,
        out_shape=[
            shape(x.shape, BF16),
            shape((2, BLOCKS, 12 * CHUNK, COLS), BF16),
            shape((8, D), F32),
            shape((1, FF), F32),
            shape((NG, WP, GH * WP), F32),
        ],
        in_specs=[VMEM] * 6,
        out_specs=[VMEM] * 5,
        scratch_shapes=[
            pltpu.VMEM((IMG_ROWS, 3 * D), BF16),
            pltpu.VMEM((IMG_ROWS, D), BF16),
            pltpu.VMEM((NW, NG, WP, GH * WP), F32),
            pltpu.VMEM((IMG_ROWS, D), BF16),
            pltpu.VMEM((tokens, D), BF16),
            pltpu.VMEM((tokens, D), BF16),
            pltpu.VMEM((tokens, D), BF16),
            pltpu.VMEM((tokens, D), BF16),
            pltpu.VMEM((tokens, D), BF16),
            pltpu.VMEM((tokens, FF), BF16),
            pltpu.VMEM((tokens, FF), BF16),
            pltpu.VMEM((tokens, 3 * D), BF16),
            pltpu.VMEM((3, D, D), BF16),
            pltpu.VMEM((D, D), BF16),
            pltpu.VMEM((D, FF), BF16),
            pltpu.VMEM((D, FF), BF16),
        ],
        compiler_params=pltpu.CompilerParams(vmem_limit_bytes=56 * 1024 * 1024),
        cost_estimate=layer_cost(images, 9),
    )(x, grad, small, fc1b, mats, bias)


def pack_shard(qkv, proj, fc1, fc2):
    rows, cols = proj.shape
    def quarters(m):
        return m.reshape(rows, FF // D, cols).transpose(1, 0, 2).reshape(-1, cols)
    return jnp.concatenate([qkv.reshape(-1, cols), proj, quarters(fc1), quarters(fc2)], axis=0)


def unpack_shard(packed, rows, cols):
    def wide(m):
        return m.reshape(FF // D, rows, cols).transpose(1, 0, 2).reshape(rows, FF // D * cols)
    return (
        packed[: 3 * rows].reshape(3, rows, cols),
        packed[3 * rows : 4 * rows],
        wide(packed[4 * rows : 8 * rows]),
        wide(packed[8 * rows :]),
    )


def to_blocks(gathered, dp, rows):
    parts = gathered.reshape(BLOCKS, dp // BLOCKS, 2, 12, rows, COLS)
    return parts.transpose(0, 2, 3, 1, 4, 5).reshape(BLOCKS, 2, 12 * CHUNK, COLS)


def from_blocks(blocks, dp, rows):
    parts = blocks.reshape(2, BLOCKS, 12, dp // BLOCKS, rows, COLS)
    return parts.transpose(0, 1, 3, 2, 4, 5).reshape(2, dp, 12 * rows, COLS)


def exchange_half(array, axis, name, bit):
    bits = [(i, i ^ (1 << bit)) for i in range(lax.axis_size(name))]
    which = (lax.axis_index(name) >> bit) & 1
    there = lax.ppermute(half_of(array, 1 - which, axis), name, bits)
    return (half_of(array, which, axis).astype(F32) + there.astype(F32)).astype(BF16)


def total_of(array, dp):
    array = array + swapped(array, "tensor")
    array = array + swapped(array, "pipe")
    for bit in range(dp.bit_length() - 1):
        array = array + lax.ppermute(array, "dp", [(i, i ^ (1 << bit)) for i in range(dp)])
    return array


def scatter_sum(blocks, dp, rows, earlier):
    array = from_blocks(blocks, dp, rows)
    array = exchange_half(array, 0, "tensor", 0)
    array, earlier = lax.optimization_barrier((array, earlier))
    levels = dp.bit_length() - 1
    array = array.reshape((2,) * levels + (2, 6 * rows, COLS))
    last = levels - 1
    done = []
    for part in range(2):
        one = array[..., part * (COLS // 2) : (part + 1) * (COLS // 2)]
        if part == 0:
            one = exchange_half(one, levels, "pipe", 0)
            one = exchange_half(one, last, "dp", 0)
        else:
            one = exchange_half(one, last, "dp", 0)
            one = exchange_half(one, levels, "pipe", 0)
        for level in range(levels - 1):
            one = exchange_half(one, level, "dp", levels - 1 - level)
        done.append(one.reshape(6 * rows, COLS // 2))
    return jnp.concatenate(done, axis=1), earlier


def swapped(array, axis):
    return lax.ppermute(array, axis, [(0, 1), (1, 0)])


def half_of(array, which, axis):
    size = array.shape[axis] // 2
    return lax.dynamic_slice_in_dim(array, which * size, size, axis)


def on_device(ends, image_counts, norm_gains, norm_shifts, w_qkv, qv_bias, rel_table, w_proj,
              out_biases, w_fc1, fc1_bias, w_fc2):
    pipe = lax.axis_index("pipe")
    tensor = lax.axis_index("tensor")
    first = pipe == 0
    dp_n = lax.axis_size("dp")
    rows, cols = w_proj.shape[1], w_proj.shape[2]

    shard = pack_shard(w_qkv[0], w_proj[0], w_fc1[0], w_fc2[0])
    kept = half_of(shard, pipe, 0)
    got = swapped(half_of(shard, 1 - pipe, 0), "pipe")
    gathered = [
        lax.all_gather(jnp.where(first, kept, got), ALL_AXES, axis=0, tiled=True),
        lax.all_gather(jnp.where(first, got, kept), ALL_AXES, axis=0, tiled=True),
    ]
    mats = [to_blocks(gathered[0], dp_n, rows)]

    heads_here = rel_table.shape[1]
    sizes = (2 * D, 2 * D, 2 * D, 2 * cols, fc1_bias.shape[1], heads_here * TABLE)
    small_local = jnp.concatenate(
        [a.reshape(-1) for a in (norm_gains, norm_shifts, out_biases, qv_bias, fc1_bias, rel_table)]
    )
    small_all = lax.all_gather(small_local, ("pipe", "tensor"), axis=0, tiled=True).reshape(2, 2, -1)
    cuts = np.cumsum((0,) + sizes)
    smalls, hidden, biases = [], [], []
    region = region_masks()
    for layer in range(2):
        mine = [small_all[layer, :, cuts[i] : cuts[i + 1]] for i in range(6)]
        gains = mine[0][0].reshape(2, D)
        shifts = mine[1][0].reshape(2, D)
        outs = mine[2][0].reshape(2, D)
        qv = mine[3].reshape(2, 2, cols).transpose(1, 0, 2).reshape(2, D)
        smalls.append(
            jnp.concatenate(
                [gains[0:1], shifts[0:1], gains[1:2], shifts[1:2], qv[0:1], qv[1:2], outs], axis=0
            )
        )
        hidden.append(mine[4].reshape(1, FF))
        table = mine[5].reshape(HEADS, TABLE)
        biases.append(score_bias(table, region if layer == 1 else region[:1] * 0.0))

    own = ends[0]
    got_rows = swapped(half_of(own, 1 - pipe, 1), "pipe")
    kept_rows = half_of(own, pipe, 1)
    both = jnp.stack([jnp.where(first, kept_rows, got_rows), jnp.where(first, got_rows, kept_rows)])

    def whole_images(part):
        mine = half_of(part, tensor, 1)
        other = swapped(half_of(part, 1 - tensor, 1), "tensor")
        return jnp.concatenate(
            [jnp.where(tensor == 0, mine, other), jnp.where(tensor == 0, other, mine)], axis=0
        )

    x_tokens, c_tokens = whole_images(both[0]), whole_images(both[1])
    images = x_tokens.shape[1]
    slots = (pipe * 2 + tensor) * images + jnp.arange(images, dtype=jnp.int32)
    real = (slots < image_counts[0]).astype(BF16)
    c_tokens = c_tokens * real[None, :, None]
    order = [one_hot_order(0), one_hot_order(SHIFT)]

    def placed(matrix, tokens, spec):
        return jnp.einsum(spec, jnp.asarray(matrix, BF16), tokens, preferred_element_type=F32).astype(BF16)

    x_in = placed(order[0], x_tokens, "rs,sbd->brd")
    c_in = placed(order[1], c_tokens, "rs,sbd->brd")

    y0 = run_forward(x_in, smalls[0], hidden[0], mats[0], biases[0])
    y0, second_mats = lax.optimization_barrier((y0, gathered[1]))
    y0 = placed(order[1] @ order[0].T, y0, "rs,bsd->brd")
    back1 = run_backward(y0, c_in, smalls[1], hidden[1], to_blocks(second_mats, dp_n, rows), biases[1])
    g_mid = placed(order[0] @ order[1].T, back1[0], "rs,bsd->brd")
    g1 = lax.psum_scatter(
        from_blocks(back1[1], dp_n, rows).reshape(-1, cols),
        ("tensor", "dp", "pipe"),
        scatter_dimension=0,
        tiled=True,
    )
    back0 = run_backward(x_in, g_mid, smalls[0], hidden[0], mats[0], biases[0])
    g0, g1 = scatter_sum(back0[1], dp_n, rows, g1)

    other = swapped(jnp.where(first, g1, g0), "pipe")
    mine = jnp.where(first, g0, g1)
    mats_grad = jnp.where(
        first, jnp.concatenate([mine, other], axis=0), jnp.concatenate([other, mine], axis=0)
    ).astype(F32)
    qkv_g, proj_g, fc1_g, fc2_g = unpack_shard(mats_grad, rows, cols)

    hot = rel_one_hot().reshape(TABLE, WP * WP)

    def small_grads(back):
        scores = back[4].reshape(NG, WP, GH, WP).transpose(0, 2, 1, 3).reshape(HEADS, WP * WP)
        table = lax.dot_general(scores, hot, (((1,), (1,)), ((), ())), precision=HIGHEST)
        return jnp.concatenate([back[2].reshape(-1), back[3].reshape(-1), table.reshape(-1)])

    summed = total_of(jnp.stack([small_grads(back0), small_grads(back1)]), dp_n)
    summed = jnp.where(first, summed[0], summed[1])
    rows_g = summed[: 8 * D].reshape(8, D)
    gains_g = jnp.stack([rows_g[0], rows_g[2]])
    shifts_g = jnp.stack([rows_g[1], rows_g[3]])
    qv_g = half_of(rows_g[4:6], tensor, 1)
    outs_g = rows_g[6:8]
    fc1b_g = half_of(summed[8 * D : 8 * D + FF], tensor, 0)
    table_g = half_of(summed[8 * D + FF :].reshape(HEADS, TABLE), tensor, 0)

    dx = placed(order[0], back0[0], "rs,brd->sbd")
    gm = placed(order[0], g_mid, "rs,brd->sbd")

    def split_rows(tokens):
        mine = half_of(tokens, tensor, 0)
        other = swapped(half_of(tokens, 1 - tensor, 0), "tensor")
        return jnp.concatenate(
            [jnp.where(tensor == 0, mine, other), jnp.where(tensor == 0, other, mine)], axis=1
        )

    dx, gm = split_rows(dx), split_rows(gm)
    other = swapped(jnp.where(first, gm, dx), "pipe")
    mine = jnp.where(first, dx, gm)
    section = jnp.where(
        first, jnp.concatenate([mine, other], axis=1), jnp.concatenate([other, mine], axis=1)
    )
    return (
        section[None],
        gains_g[None],
        shifts_g[None],
        qkv_g[None],
        qv_g[None],
        table_g[None],
        proj_g[None],
        outs_g[None],
        fc1_g[None],
        fc1b_g[None],
        fc2_g[None],
    )


def solution(mesh):
    return jax.shard_map(
        on_device,
        mesh=mesh,
        in_specs=(
            P("pipe", "tensor", "dp", None),
            P("dp"),
            P("pipe", None, None),
            P("pipe", None, None),
            P("pipe", None, "dp", "tensor"),
            P("pipe", None, "tensor"),
            P("pipe", "tensor", None),
            P("pipe", "dp", "tensor"),
            P("pipe", None, None),
            P("pipe", "dp", "tensor"),
            P("pipe", "tensor"),
            P("pipe", "dp", "tensor"),
        ),
        out_specs=(
            P("pipe", "tensor", "dp", None),
            P("pipe", None, None),
            P("pipe", None, None),
            P("pipe", None, "dp", "tensor"),
            P("pipe", None, "tensor"),
            P("pipe", "tensor", None),
            P("pipe", "dp", "tensor"),
            P("pipe", None, None),
            P("pipe", "dp", "tensor"),
            P("pipe", "tensor"),
            P("pipe", "dp", "tensor"),
        ),
        check_vma=False,
    )
```
